32 devices in a mesh: dp: 8 (over z, x), expert: 4 (over y, core).
Axes of the slice: x: 2, y: 2, z: 4, core: 2. Of those that a mesh axis runs over, the one named last changes fastest.
Arguments:
- step_inputs: bfloat16 [4096, 2048], P(('dp', 'expert')), may hold values from -6 to 6
- step_cotangent: bfloat16 [4096, 2048], P(('dp', 'expert')), may hold values from -6 to 6
- step_routes: int32 [4096, 1], P(('dp', 'expert')), may hold values from 0 to 3; in each aligned block of 128 rows (0 to 127, 128 to 255, ...) at most 40 rows name the same one
- step_gates: float32 [4096, 1], P(('dp', 'expert')), may hold values from 0.1 to 1
- next_inputs: bfloat16 [4096, 2048], P(('dp', 'expert')), may hold values from -6 to 6
- next_routes: int32 [4096, 1], P(('dp', 'expert')), may hold values from 0 to 3; in each aligned block of 128 rows (0 to 127, 128 to 255, ...) at most 40 rows name the same one
- next_gates: float32 [4096, 1], P(('dp', 'expert')), may hold values from 0.1 to 1
- master_weights: float32 [4, 2048, 3456], P('expert', 'dp'), may hold values from -4 to 4
- first_moment: float32 [4, 2048, 3456], P('expert', 'dp'), may hold values from -0.6 to 0.6
- second_moment: float32 [4, 2048, 3456], P('expert', 'dp'), may hold values from 0.01 to 0.2
- owner_plan: int32 [4], replicated, may hold values from 0 to 3, as said below
Outputs:
- layer_output: bfloat16 [4096, 2048], P(('dp', 'expert'))
- moved_weights: float32 [4, 2048, 3456], P('expert', 'dp')
- moved_first: float32 [4, 2048, 3456], P('expert', 'dp')
- moved_second: float32 [4, 2048, 3456], P('expert', 'dp')
The draws below stay inside these ranges and needn't reach their ends.
Inputs may be any that keep to these rules, and one draw needn't show every extreme that they name: `step_routes`: among the 128 tokens of one device no expert is named more than 40 times. `next_routes`: among the 128 tokens of one device no expert is named more than 40 times. `owner_plan`: every index appears once.
All inputs are finite; a program needn't handle non-finite values.
Results may differ from the reference program's by a relative error of at most 0.025.
Values may be sent and summed in bfloat16 or wider, within the bound.
A program may use at most 128 MiB of HBM per device.

```python
import math
from functools import partial
import jax
import jax.numpy as jnp
import numpy as np
from jax import lax

D = 2048
HID = 1152
EXPERTS = 4
TOPK = 1
TOK_DEV = 128
SPLIT = 1
HID_DEV = 1152
SLABS = 4
CAP = 40
TOKENS = 4096
N_DP = 8
N_EXPERT = 4


def draw_owner_plan(key, part):
    mixed = jax.random.fold_in(key, 7919)
    return jax.random.permutation(mixed, SLABS).astype(jnp.int32)


def levels(key, extent, shards, low, largest):
    factor_of, own = 1.0, jax.random.fold_in(key, 6)
    for axis_at, parts in shards:
        heights = jnp.exp(jax.random.uniform(jax.random.fold_in(own, axis_at), (parts,), jnp.float32, low / len(shards), largest / len(shards)))
        factor_of = factor_of * jnp.repeat(heights, extent[axis_at] // parts).reshape([-1 if axis == axis_at else 1 for axis in range(len(extent))])
    return factor_of


def deal_out(stream_key, own, number, rows, count, top, limit, skew):
    sequence = jax.random.permutation(stream_key, count)
    packed, usual = load_shares(count, rows * top, limit, skew, True), load_shares(count, rows * top, limit, skew, False)
    places = jnp.arange(count)

    def named(tallies, offset_by):
        used = int((tallies > 0).sum())
        fixed = max(1, used // 4)
        shifted = fixed + (places - fixed + offset_by * (used - fixed)) % max(1, count - fixed)
        return jnp.zeros((count,), jnp.int32).at[sequence[jnp.where(places < fixed, places, shifted)]].set(jnp.asarray(tallies, jnp.int32))

    tallies = jnp.where(number % 4 == 0, named(packed, number // 4), named(usual, number - number // 4 - 1))
    mixed = jax.random.permutation(jax.random.fold_in(own, 3), count)
    giver, taker = mixed[0:count // 2 * 2:2], mixed[1:count // 2 * 2:2]
    slack = jnp.minimum(tallies[giver] - 1, limit - tallies[taker]) // 2
    slack = jnp.where((giver == sequence[0]) | (taker == sequence[0]) | (tallies[taker] == 0), 0, jnp.maximum(slack, 0))
    shifted = jax.random.randint(jax.random.fold_in(own, 4), (count // 2,), 0, 1 << 20) % (slack + 1)
    tallies = tallies.at[giver].add(-shifted).at[taker].add(shifted)
    labels = jnp.searchsorted(jnp.cumsum(tallies), jnp.arange(rows * top), side="right").astype(jnp.int32)
    grid = labels.reshape(top, rows).T
    grid = grid[jax.random.permutation(jax.random.fold_in(own, 1), rows)]
    offset_by = jax.random.randint(jax.random.fold_in(own, 2), (rows, 1), 0, top)
    return jnp.take_along_axis(grid, (jnp.arange(top)[None, :] + offset_by) % top, axis=1)


def load_shares(count, total, most, slope, full):
    portions = [(1 << 20) // math.isqrt(rank ** slope) + 1 for rank in range(1, count + 1)]
    largest = most if full else min(most, max(-(-total // count), total * portions[0] // sum(portions)))
    least = 1 if total - largest >= count - 1 else 0
    holding, spare = [largest] + [least] * (count - 1), total - largest - least * (count - 1)
    while spare > 0:
        candidates = [i for i in range(1, count) if holding[i] < largest] or [i for i in range(1, count) if holding[i] < most]
        whole, remaining = sum([portions[i] for i in candidates]), spare
        for i in candidates:
            more = min(most - holding[i], max(1, remaining * portions[i] // whole), spare)
            holding[i] = holding[i] + more
            spare = spare - more
    return np.array(holding)


def gaussian(rng, shape, scale, bound, split=(), kind=jnp.bfloat16):
    drawn = jax.random.normal(rng, shape, jnp.float32) * scale
    if len(split) > 0:
        drawn = levels(rng, shape, split, -0.22, 0.18) * drawn
    return jnp.clip(drawn, min=-bound, max=bound).astype(kind)


def setup_inputs(seed: int = 0) -> dict:
    key_list = jax.random.split(jax.random.key(seed), 12)
    step_inputs = gaussian(key_list[0], (TOKENS, D), 1.0, 6.0, ((0, 32),))
    step_cotangent = gaussian(key_list[1], (TOKENS, D), 1.0, 6.0, ((0, 32),))
    step_routes_keys = jax.random.split(jax.random.fold_in(key_list[2], 1), TOKENS // TOK_DEV)
    step_routes_turns = jax.random.permutation(jax.random.fold_in(key_list[2], 3), TOKENS // TOK_DEV)
    step_routes = jax.vmap(lambda own, number: deal_out(jax.random.fold_in(key_list[2], 2), own, number, TOK_DEV, EXPERTS, TOPK, CAP, 2))(step_routes_keys, step_routes_turns).reshape((TOKENS, TOPK))
    step_gates = jnp.clip(0.1 + 0.9 * jax.random.uniform(key_list[3], (TOKENS, TOPK), jnp.float32) ** levels(key_list[3], (TOKENS, TOPK), ((0, 32),), -0.2, 0.2), 0.1, 1.0)
    next_inputs = gaussian(key_list[4], (TOKENS, D), 1.0, 6.0, ((0, 32),))
    next_routes_keys = jax.random.split(jax.random.fold_in(key_list[5], 1), TOKENS // TOK_DEV)
    next_routes_turns = jax.random.permutation(jax.random.fold_in(key_list[5], 3), TOKENS // TOK_DEV)
    next_routes = jax.vmap(lambda own, number: deal_out(jax.random.fold_in(key_list[5], 2), own, number, TOK_DEV, EXPERTS, TOPK, CAP, 2))(next_routes_keys, next_routes_turns).reshape((TOKENS, TOPK))
    next_gates = jnp.clip(0.1 + 0.9 * jax.random.uniform(key_list[6], (TOKENS, TOPK), jnp.float32) ** levels(key_list[6], (TOKENS, TOPK), ((0, 32),), -0.2, 0.2), 0.1, 1.0)
    master_weights = gaussian(key_list[7], (SLABS, D, 3 * HID_DEV), 1.0, 4.0, ((0, 4), (1, 8)), jnp.float32)
    first_moment = gaussian(key_list[8], (SLABS, D, 3 * HID_DEV), 0.1, 0.6, ((0, 4), (1, 8)), jnp.float32)
    second_moment = jnp.clip(jnp.exp(math.log(0.2) - 2.9957323 * jax.random.uniform(key_list[9], (SLABS, D, 3 * HID_DEV), jnp.float32) ** levels(key_list[9], (SLABS, D, 3 * HID_DEV), ((0, 4), (1, 8)), -0.2, 0.2)), 0.01, 0.2)
    owner_plan = draw_owner_plan(jax.random.fold_in(key_list[11], 71), 0)
    return {"step_inputs": step_inputs, "step_cotangent": step_cotangent, "step_routes": step_routes, "step_gates": step_gates, "next_inputs": next_inputs, "next_routes": next_routes, "next_gates": next_gates, "master_weights": master_weights, "first_moment": first_moment, "second_moment": second_moment, "owner_plan": owner_plan}


beta_one = 0.9
beta_two = 0.95
learn_rate = 0.2
decay_rate = 0.1
adam_step = 10.0
adam_eps = 1e-08

def slot_targets(routes, capacity):
    pair_ids = routes.reshape(-1).astype(jnp.int32)
    one_hot = (pair_ids[:, None] == jnp.arange(EXPERTS, dtype=jnp.int32)[None, :]).astype(jnp.int32)
    earlier = jnp.cumsum(one_hot, axis=0) - one_hot
    slot_ids = lax.optimization_barrier(jnp.sum(earlier * one_hot, axis=1)).astype(jnp.int32)
    return pair_ids * capacity + slot_ids

def dispatch(routes, payload):
    targets = slot_targets(routes, CAP)
    filled = jnp.zeros((EXPERTS * CAP, payload.shape[1]), payload.dtype).at[targets].set(payload)
    return filled.reshape(EXPERTS, CAP, payload.shape[1])

def reference(step_inputs, step_cotangent, step_routes, step_gates, next_inputs, next_routes, next_gates, master_weights, first_moment, second_moment, owner_plan):
    blocks = N_DP * N_EXPERT
    width = HID_DEV
    in_scale = D ** (-0.5)
    out_scale = HID ** (-0.5)
    pair_count = TOK_DEV * TOPK
    step_blocks = step_routes.reshape(blocks, TOK_DEV, TOPK)
    input_pairs = jnp.repeat(step_inputs, TOPK, axis=0).reshape(blocks, pair_count, D)
    scaled_pairs = (jnp.repeat(step_cotangent, TOPK, axis=0).astype(jnp.float32) * step_gates.reshape(-1, 1)).astype(jnp.bfloat16)
    scaled_pairs = scaled_pairs.reshape(blocks, pair_count, D)
    sent_inputs = jax.vmap(dispatch)(step_blocks, input_pairs)
    sent_scaled = jax.vmap(dispatch)(step_blocks, scaled_pairs)
    compute_weights = master_weights.astype(jnp.bfloat16)

    def slab_gradient(slab_index):
        expert = slab_index // SPLIT
        inputs_rows = jnp.take(sent_inputs, expert, axis=1).reshape(-1, D)
        scaled_rows = jnp.take(sent_scaled, expert, axis=1).reshape(-1, D)
        weights = jnp.take(compute_weights, slab_index, axis=0)
        gate_pre = jnp.dot(inputs_rows, weights[:, :width], preferred_element_type=jnp.float32) * in_scale
        up_pre = jnp.dot(inputs_rows, weights[:, width:2 * width], preferred_element_type=jnp.float32) * in_scale
        down_back = jnp.dot(scaled_rows, weights[:, 2 * width:], preferred_element_type=jnp.float32) * out_scale
        sigmoid_gate = jax.nn.sigmoid(gate_pre)
        silu_gate = gate_pre * sigmoid_gate
        activation = (silu_gate * up_pre).astype(jnp.bfloat16)
        gate_grad = (down_back * up_pre * sigmoid_gate * (1.0 + gate_pre * (1.0 - sigmoid_gate))).astype(jnp.bfloat16)
        up_grad = (down_back * silu_gate).astype(jnp.bfloat16)
        inputs_groups = inputs_rows.reshape(N_DP, -1, D).astype(jnp.float32)
        scaled_groups = scaled_rows.reshape(N_DP, -1, D).astype(jnp.float32)
        gate_part = jnp.einsum('nrd,nrh->ndh', inputs_groups, gate_grad.reshape(N_DP, -1, width).astype(jnp.float32), precision=lax.Precision.HIGHEST) * in_scale
        up_part = jnp.einsum('nrd,nrh->ndh', inputs_groups, up_grad.reshape(N_DP, -1, width).astype(jnp.float32), precision=lax.Precision.HIGHEST) * in_scale
        down_part = jnp.einsum('nrd,nrh->ndh', scaled_groups, activation.reshape(N_DP, -1, width).astype(jnp.float32), precision=lax.Precision.HIGHEST) * out_scale
        partial_grad = jnp.concatenate([gate_part, up_part, down_part], axis=2).astype(jnp.bfloat16)
        return lax.optimization_barrier(jnp.sum(partial_grad.astype(jnp.float32), axis=0))
    gradient = lax.map(slab_gradient, jnp.arange(SLABS, dtype=jnp.int32))
    first_new = beta_one * first_moment + (1.0 - beta_one) * gradient
    second_new = beta_two * second_moment + (1.0 - beta_two) * gradient * gradient
    first_hat = first_new / (1.0 - beta_one ** adam_step)
    second_hat = second_new / (1.0 - beta_two ** adam_step)
    weights_new = master_weights - learn_rate * (first_hat / (jnp.sqrt(second_hat) + adam_eps) + decay_rate * master_weights)
    moved_weights = jnp.zeros_like(weights_new).at[owner_plan].set(weights_new)
    moved_first = jnp.zeros_like(first_new).at[owner_plan].set(first_new)
    moved_second = jnp.zeros_like(second_new).at[owner_plan].set(second_new)
    next_blocks = next_routes.reshape(blocks, TOK_DEV, TOPK)
    next_pairs = jnp.repeat(next_inputs, TOPK, axis=0).reshape(blocks, pair_count, D)
    sent_next = jax.vmap(dispatch)(next_blocks, next_pairs)
    next_targets = jax.vmap(partial(slot_targets, capacity=CAP))(next_blocks)
    pair_expert = (next_targets // CAP).reshape(-1)
    pair_rows = (jnp.arange(blocks, dtype=jnp.int32)[:, None] * CAP + next_targets % CAP).reshape(-1).astype(jnp.int32)
    serve_weights = weights_new.astype(jnp.bfloat16)

    def add_slab(running, slab_index):
        expert = slab_index // SPLIT
        weights = jnp.take(serve_weights, slab_index, axis=0)
        rows_in = jnp.take(sent_next, expert, axis=1).reshape(-1, D)
        gate_pre = jnp.dot(rows_in, weights[:, :width], preferred_element_type=jnp.float32) * in_scale
        up_pre = jnp.dot(rows_in, weights[:, width:2 * width], preferred_element_type=jnp.float32) * in_scale
        activation = (gate_pre * jax.nn.sigmoid(gate_pre) * up_pre).astype(jnp.bfloat16)
        slab_partial = (lax.dot_general(activation, weights[:, 2 * width:], (((1,), (1,)), ((), ())), preferred_element_type=jnp.float32) * out_scale).astype(jnp.bfloat16)
        picked = jnp.take(slab_partial, pair_rows, axis=0).astype(jnp.float32)
        chosen = pair_expert == expert
        return (running + jnp.where(chosen[:, None], picked, jnp.zeros_like(picked)), None)
    pair_sums, unused = lax.scan(add_slab, jnp.zeros((blocks * pair_count, D), jnp.float32), jnp.arange(SLABS, dtype=jnp.int32))
    weighted = pair_sums * next_gates.reshape(-1, 1)
    layer_output = lax.optimization_barrier(jnp.sum(weighted.reshape(-1, TOPK, D), axis=1)).astype(jnp.bfloat16)
    return (layer_output, moved_weights, moved_first, moved_second)
```

```python
import jax
import jax.numpy as jnp
from jax import lax
from jax.sharding import PartitionSpec as P

D = 2048
HID = 1152
EXPERTS = 4
CAP = 40


beta_one = 0.9
beta_two = 0.95
learn_rate = 0.2
decay_rate = 0.1
adam_step = 10.0
adam_eps = 1e-08


def slot_targets(routes, capacity):
    pair_ids = routes.reshape(-1)
    count = pair_ids.shape[0]
    before = lax.broadcasted_iota(jnp.int32, (count, count), 1) < lax.broadcasted_iota(
        jnp.int32, (count, count), 0
    )
    same = pair_ids[:, None] == pair_ids[None, :]
    slot_ids = jnp.sum(jnp.where(before & same, 1, 0), axis=1, dtype=jnp.int32)
    return pair_ids * capacity + slot_ids


def exchange(array, axis):
    return lax.all_to_all(array, axis, split_axis=0, concat_axis=0, tiled=True)


def hidden_terms(gate_pre, up_pre, down_back):
    sigmoid_gate = jax.nn.sigmoid(gate_pre)
    silu_gate = gate_pre * sigmoid_gate
    activation = (silu_gate * up_pre).astype(jnp.bfloat16)
    gate_grad = (
        down_back * up_pre * sigmoid_gate * (1.0 + gate_pre * (1.0 - sigmoid_gate))
    ).astype(jnp.bfloat16)
    up_grad = (down_back * silu_gate).astype(jnp.bfloat16)
    return activation, gate_grad, up_grad


def gradient_by_weights(flat_inputs, flat_scaled, old_weights, width, in_scale, out_scale):
    piece = lax.all_gather(old_weights.astype(jnp.bfloat16), "dp", axis=0, tiled=True)
    gate_pre = jnp.dot(flat_inputs, piece[:, :width], preferred_element_type=jnp.float32) * in_scale
    up_pre = (
        jnp.dot(flat_inputs, piece[:, width : 2 * width], preferred_element_type=jnp.float32)
        * in_scale
    )
    down_back = (
        jnp.dot(flat_scaled, piece[:, 2 * width :], preferred_element_type=jnp.float32) * out_scale
    )
    activation, gate_grad, up_grad = hidden_terms(gate_pre, up_pre, down_back)
    contract = (((0,), (0,)), ((), ()))
    parts = [
        lax.dot_general(rows, terms, contract, preferred_element_type=jnp.float32) * scale
        for rows, terms, scale in (
            (flat_inputs, gate_grad, in_scale),
            (flat_inputs, up_grad, in_scale),
            (flat_scaled, activation, out_scale),
        )
    ]
    return lax.psum_scatter(
        jnp.concatenate(parts, axis=1).astype(jnp.bfloat16),
        "dp",
        scatter_dimension=0,
        tiled=True,
    ).astype(jnp.float32)


def gradient_by_tokens(flat_inputs, flat_scaled, old_weights, width, in_scale, out_scale):
    shards_dp = lax.axis_size("dp")
    depth = old_weights.shape[0]
    columns = width // shards_dp
    all_inputs = lax.all_gather(flat_inputs, "dp", axis=0, tiled=True)
    all_scaled = lax.all_gather(flat_scaled, "dp", axis=0, tiled=True)
    turned = old_weights.astype(jnp.bfloat16).T.reshape(3, shards_dp, columns, depth)
    mine = exchange(turned.transpose(1, 0, 2, 3), "dp")
    mine = mine.transpose(1, 2, 0, 3).reshape(3 * columns, shards_dp * depth)
    contract = (((1,), (1,)), ((), ()))
    gate_up = (
        lax.dot_general(
            mine[: 2 * columns], all_inputs, contract, preferred_element_type=jnp.float32
        )
        * in_scale
    )
    down_back = (
        lax.dot_general(
            mine[2 * columns :], all_scaled, contract, preferred_element_type=jnp.float32
        )
        * out_scale
    )
    activation, gate_grad, up_grad = hidden_terms(gate_up[:columns], gate_up[columns:], down_back)
    gate_up_part = (
        jnp.dot(
            jnp.concatenate([gate_grad, up_grad], axis=0),
            all_inputs,
            preferred_element_type=jnp.float32,
        )
        * in_scale
    )
    down_part = jnp.dot(activation, all_scaled, preferred_element_type=jnp.float32) * out_scale
    grads = jnp.concatenate([gate_up_part.astype(jnp.bfloat16), down_part.astype(jnp.bfloat16)], axis=0)
    grads = grads.reshape(3, columns, shards_dp, depth).transpose(2, 0, 1, 3)
    back = exchange(grads, "dp").transpose(1, 0, 2, 3).reshape(3 * width, depth)
    return back.T.astype(jnp.float32)


def forward_by_weights(flat_rows, new_weights, width, in_scale, out_scale):
    full = lax.all_gather(new_weights, "dp", axis=0, tiled=True)
    gate = jnp.dot(flat_rows, full[:, :width], preferred_element_type=jnp.float32) * in_scale
    up = (
        jnp.dot(flat_rows, full[:, width : 2 * width], preferred_element_type=jnp.float32)
        * in_scale
    )
    activation = (gate * jax.nn.sigmoid(gate) * up).astype(jnp.bfloat16)
    return (
        lax.dot_general(
            activation,
            full[:, 2 * width :],
            (((1,), (1,)), ((), ())),
            preferred_element_type=jnp.float32,
        )
        * out_scale
    ).astype(jnp.bfloat16)


def forward_by_tokens(flat_rows, new_weights, width, in_scale, out_scale):
    shards_dp = lax.axis_size("dp")
    depth = new_weights.shape[0]
    count = flat_rows.shape[0]
    slices = exchange(flat_rows.reshape(count, shards_dp, depth).transpose(1, 0, 2), "dp")
    slices = slices.reshape(shards_dp * count, depth)
    partial_pre = (
        jnp.dot(slices, new_weights[:, : 2 * width], preferred_element_type=jnp.float32) * in_scale
    ).astype(jnp.bfloat16)
    pre = lax.psum_scatter(partial_pre, "dp", scatter_dimension=0, tiled=True).astype(jnp.float32)
    gate, up = pre[:, :width], pre[:, width:]
    activation = (gate * jax.nn.sigmoid(gate) * up).astype(jnp.bfloat16)
    gathered = lax.all_gather(activation, "dp", axis=0, tiled=True)
    out = (
        lax.dot_general(
            gathered,
            new_weights[:, 2 * width :],
            (((1,), (1,)), ((), ())),
            preferred_element_type=jnp.float32,
        )
        * out_scale
    ).astype(jnp.bfloat16)
    back = exchange(out.reshape(shards_dp, count, depth), "dp")
    return back.transpose(1, 0, 2).reshape(count, shards_dp * depth)


def dispatch_pairs(targets, payload, capacity):
    selector = (
        lax.broadcasted_iota(jnp.int32, (EXPERTS * capacity, targets.shape[0]), 0)
        == targets[None, :]
    ).astype(jnp.bfloat16)
    filled = jnp.dot(selector, payload, preferred_element_type=jnp.float32).astype(jnp.bfloat16)
    return filled.reshape(EXPERTS, capacity, payload.shape[1])


def shards(
    step_inputs,
    step_cotangent,
    step_routes,
    step_gates,
    next_inputs,
    next_routes,
    next_gates,
    master_weights,
    first_moment,
    second_moment,
    owner_plan,
):
    groups = lax.axis_size("expert")
    split = groups // EXPERTS
    width = master_weights.shape[2] // 3
    in_scale = D ** (-0.5)
    out_scale = HID ** (-0.5)
    topk_count = step_routes.shape[1]
    step_targets = slot_targets(step_routes, CAP)
    input_pairs = jnp.repeat(step_inputs, topk_count, axis=0)
    scaled_pairs = (
        jnp.repeat(step_cotangent, topk_count, axis=0).astype(jnp.float32) * step_gates
    ).astype(jnp.bfloat16)
    send_inputs = jnp.repeat(dispatch_pairs(step_targets, input_pairs, CAP), split, axis=0)
    send_scaled = jnp.repeat(dispatch_pairs(step_targets, scaled_pairs, CAP), split, axis=0)
    flat_inputs = exchange(send_inputs, "expert").reshape(-1, D)
    flat_scaled = exchange(send_scaled, "expert").reshape(-1, D)
    old_weights = master_weights[0]
    shards_dp = lax.axis_size("dp")
    by_tokens = 2 * shards_dp * flat_inputs.shape[0] <= 3 * width and width % shards_dp == 0
    gradient = (gradient_by_tokens if by_tokens else gradient_by_weights)(
        flat_inputs, flat_scaled, old_weights, width, in_scale, out_scale
    )
    first_new = beta_one * first_moment[0] + (1.0 - beta_one) * gradient
    second_new = beta_two * second_moment[0] + (1.0 - beta_two) * gradient * gradient
    first_hat = first_new / (1.0 - beta_one**adam_step)
    second_hat = second_new / (1.0 - beta_two**adam_step)
    new_weights = old_weights - learn_rate * (
        first_hat / (jnp.sqrt(second_hat) + adam_eps) + decay_rate * old_weights
    )
    positions = jnp.arange(groups, dtype=jnp.int32)
    holder = jnp.sum(
        jnp.where(owner_plan[:, None] == positions[None, :], positions[:, None], 0), axis=0
    )
    stacked = jnp.stack([new_weights, first_new, second_new])
    rows_here = stacked.shape[1]
    pieces = stacked.reshape(3, groups, rows_here // groups, stacked.shape[2])
    spread = lax.all_to_all(
        pieces.astype(jnp.bfloat16), "expert", split_axis=1, concat_axis=1, tiled=True
    ).astype(pieces.dtype)
    ordered = jnp.concatenate(
        [lax.dynamic_slice_in_dim(spread, holder[p], 1, axis=1) for p in range(groups)], axis=1
    )
    collected = lax.all_to_all(
        ordered.astype(jnp.bfloat16), "expert", split_axis=1, concat_axis=1, tiled=True
    ).astype(ordered.dtype)
    relocated = collected.reshape(3, rows_here, stacked.shape[2])
    next_targets = slot_targets(next_routes, CAP)
    next_pairs = jnp.repeat(next_inputs, topk_count, axis=0)
    send_next = jnp.repeat(dispatch_pairs(next_targets, next_pairs, CAP), split, axis=0)
    received = exchange(send_next, "expert")
    flat_rows = received.reshape(-1, D)
    partials = (forward_by_tokens if by_tokens else forward_by_weights)(
        flat_rows, new_weights.astype(jnp.bfloat16), width, in_scale, out_scale
    )
    returned = exchange(partials.reshape(received.shape), "expert").reshape(-1, D)
    places = lax.broadcasted_iota(jnp.int32, (next_targets.shape[0], groups * CAP), 1)
    selector = (
        next_targets[:, None] == (places // (split * CAP)) * CAP + places % CAP
    ).astype(jnp.bfloat16)
    pair_sums = jnp.dot(selector, returned, preferred_element_type=jnp.float32)
    weighted = pair_sums * next_gates
    layer_output = jnp.sum(weighted.reshape(-1, topk_count, D), axis=1).astype(jnp.bfloat16)
    return (layer_output, relocated[0][None], relocated[1][None], relocated[2][None])


def solution(mesh):
    placed = (
        P(("dp", "expert"), None),
        P(("dp", "expert"), None),
        P(("dp", "expert"), None),
        P(("dp", "expert"), None),
        P(("dp", "expert"), None),
        P(("dp", "expert"), None),
        P(("dp", "expert"), None),
        P("expert", "dp", None),
        P("expert", "dp", None),
        P("expert", "dp", None),
        P(),
    )
    return jax.shard_map(
        shards,
        mesh=mesh,
        in_specs=placed,
        out_specs=(
            P(("dp", "expert"), None),
            P("expert", "dp", None),
            P("expert", "dp", None),
            P("expert", "dp", None),
        ),
        check_vma=False,
    )
```

```python
import jax
import jax.numpy as jnp
from jax import lax
from jax.experimental.layout import Layout, with_layout_constraint
from jax.sharding import PartitionSpec as P

D = 2048
HID = 1152
EXPERTS = 4
CAP = 40


beta_one = 0.9
beta_two = 0.95
learn_rate = 0.2
decay_rate = 0.1
adam_step = 10.0
adam_eps = 1e-08


def slot_targets(routes, capacity):
    pair_ids = routes.reshape(-1)
    count = pair_ids.shape[0]
    before = lax.broadcasted_iota(jnp.int32, (count, count), 1) < lax.broadcasted_iota(
        jnp.int32, (count, count), 0
    )
    same = pair_ids[:, None] == pair_ids[None, :]
    slot_ids = jnp.sum(jnp.where(before & same, 1, 0), axis=1, dtype=jnp.int32)
    return pair_ids * capacity + slot_ids


def exchange(array, axis):
    return lax.all_to_all(array, axis, split_axis=0, concat_axis=0, tiled=True)


def hidden_terms(gate_pre, up_pre, down_back):
    sigmoid_gate = jax.nn.sigmoid(gate_pre)
    silu_gate = gate_pre * sigmoid_gate
    activation = (silu_gate * up_pre).astype(jnp.bfloat16)
    gate_grad = (
        down_back * up_pre * sigmoid_gate * (1.0 + gate_pre * (1.0 - sigmoid_gate))
    ).astype(jnp.bfloat16)
    up_grad = (down_back * silu_gate).astype(jnp.bfloat16)
    return activation, gate_grad, up_grad


def gradient_by_weights(flat_inputs, flat_scaled, old_weights, width, in_scale, out_scale):
    piece = lax.all_gather(old_weights.astype(jnp.bfloat16), "dp", axis=0, tiled=True)
    gate_pre = jnp.dot(flat_inputs, piece[:, :width], preferred_element_type=jnp.float32) * in_scale
    up_pre = (
        jnp.dot(flat_inputs, piece[:, width : 2 * width], preferred_element_type=jnp.float32)
        * in_scale
    )
    down_back = (
        jnp.dot(flat_scaled, piece[:, 2 * width :], preferred_element_type=jnp.float32) * out_scale
    )
    activation, gate_grad, up_grad = hidden_terms(gate_pre, up_pre, down_back)
    contract = (((0,), (0,)), ((), ()))
    parts = [
        lax.dot_general(rows, terms, contract, preferred_element_type=jnp.float32) * scale
        for rows, terms, scale in (
            (flat_inputs, gate_grad, in_scale),
            (flat_inputs, up_grad, in_scale),
            (flat_scaled, activation, out_scale),
        )
    ]
    return lax.psum_scatter(
        jnp.concatenate(parts, axis=1).astype(jnp.bfloat16),
        "dp",
        scatter_dimension=0,
        tiled=True,
    ).astype(jnp.float32)


def gradient_by_tokens(flat_inputs, flat_scaled, old_weights, width, in_scale, out_scale):
    shards_dp = lax.axis_size("dp")
    depth = old_weights.shape[0]
    columns = width // shards_dp
    all_inputs = lax.all_gather(flat_inputs, "dp", axis=0, tiled=True)
    all_scaled = lax.all_gather(flat_scaled, "dp", axis=0, tiled=True)
    rounded = with_layout_constraint(old_weights.astype(jnp.bfloat16), Layout((0, 1)))
    turned = rounded.T.reshape(3, shards_dp, columns, depth)
    mine = exchange(turned.transpose(1, 0, 2, 3), "dp")
    mine = mine.transpose(1, 2, 0, 3).reshape(3 * columns, shards_dp * depth)
    contract = (((1,), (1,)), ((), ()))
    gate_up = (
        lax.dot_general(
            mine[: 2 * columns], all_inputs, contract, preferred_element_type=jnp.float32
        )
        * in_scale
    )
    down_back = (
        lax.dot_general(
            mine[2 * columns :], all_scaled, contract, preferred_element_type=jnp.float32
        )
        * out_scale
    )
    activation, gate_grad, up_grad = hidden_terms(gate_up[:columns], gate_up[columns:], down_back)
    gate_up_part = (
        jnp.dot(
            jnp.concatenate([gate_grad, up_grad], axis=0),
            all_inputs,
            preferred_element_type=jnp.float32,
        )
        * in_scale
    )
    down_part = jnp.dot(activation, all_scaled, preferred_element_type=jnp.float32) * out_scale
    grads = jnp.concatenate([gate_up_part.astype(jnp.bfloat16), down_part.astype(jnp.bfloat16)], axis=0)
    grads = grads.reshape(3, columns, shards_dp, depth).transpose(2, 0, 1, 3)
    back = exchange(grads, "dp").transpose(1, 0, 2, 3).reshape(3 * width, depth)
    return with_layout_constraint(back.T, Layout((0, 1))).astype(jnp.float32)


def forward_by_weights(flat_rows, new_weights, beside, width, in_scale, out_scale):
    full = lax.all_gather(new_weights, "dp", axis=0, tiled=True)
    gate = jnp.dot(flat_rows, full[:, :width], preferred_element_type=jnp.float32) * in_scale
    up = (
        jnp.dot(flat_rows, full[:, width : 2 * width], preferred_element_type=jnp.float32)
        * in_scale
    )
    activation = (gate * jax.nn.sigmoid(gate) * up).astype(jnp.bfloat16)
    return (
        lax.dot_general(
            activation,
            full[:, 2 * width :],
            (((1,), (1,)), ((), ())),
            preferred_element_type=jnp.float32,
        )
        * out_scale
    ).astype(jnp.bfloat16), beside


def forward_by_tokens(flat_rows, new_weights, beside, width, in_scale, out_scale):
    shards_dp = lax.axis_size("dp")
    depth = new_weights.shape[0]
    count = flat_rows.shape[0]
    slices = exchange(flat_rows.reshape(count, shards_dp, depth).transpose(1, 0, 2), "dp")
    slices = slices.reshape(shards_dp * count, depth)
    partial_pre = (
        jnp.dot(slices, new_weights[:, : 2 * width], preferred_element_type=jnp.float32) * in_scale
    ).astype(jnp.bfloat16)
    pre = lax.psum_scatter(partial_pre, "dp", scatter_dimension=0, tiled=True).astype(jnp.float32)
    gate, up = pre[:, :width], pre[:, width:]
    activation = (gate * jax.nn.sigmoid(gate) * up).astype(jnp.bfloat16)
    activation, beside = lax.optimization_barrier((activation, beside))
    gathered = lax.all_gather(activation, "dp", axis=0, tiled=True)
    out = (
        lax.dot_general(
            gathered,
            new_weights[:, 2 * width :],
            (((1,), (1,)), ((), ())),
            preferred_element_type=jnp.float32,
        )
        * out_scale
    ).astype(jnp.bfloat16)
    back = exchange(out.reshape(shards_dp, count, depth), "dp")
    return back.transpose(1, 0, 2).reshape(count, shards_dp * depth), beside


def dispatch_pairs(targets, payload, capacity):
    selector = (
        lax.broadcasted_iota(jnp.int32, (EXPERTS * capacity, targets.shape[0]), 0)
        == targets[None, :]
    ).astype(jnp.bfloat16)
    filled = jnp.dot(selector, payload, preferred_element_type=jnp.float32).astype(jnp.bfloat16)
    return filled.reshape(EXPERTS, capacity, payload.shape[1])


def shards(
    step_inputs,
    step_cotangent,
    step_routes,
    step_gates,
    next_inputs,
    next_routes,
    next_gates,
    master_weights,
    first_moment,
    second_moment,
    owner_plan,
):
    groups = lax.axis_size("expert")
    split = groups // EXPERTS
    width = master_weights.shape[2] // 3
    in_scale = D ** (-0.5)
    out_scale = HID ** (-0.5)
    topk_count = step_routes.shape[1]
    step_targets = slot_targets(step_routes, CAP)
    input_pairs = jnp.repeat(step_inputs, topk_count, axis=0)
    scaled_pairs = (
        jnp.repeat(step_cotangent, topk_count, axis=0).astype(jnp.float32) * step_gates
    ).astype(jnp.bfloat16)
    send_inputs = jnp.repeat(dispatch_pairs(step_targets, input_pairs, CAP), split, axis=0)
    send_scaled = jnp.repeat(dispatch_pairs(step_targets, scaled_pairs, CAP), split, axis=0)
    flat_inputs = exchange(send_inputs, "expert").reshape(-1, D)
    flat_scaled = exchange(send_scaled, "expert").reshape(-1, D)
    old_weights = master_weights[0]
    shards_dp = lax.axis_size("dp")
    by_tokens = 2 * shards_dp * flat_inputs.shape[0] <= 3 * width and width % shards_dp == 0
    gradient = (gradient_by_tokens if by_tokens else gradient_by_weights)(
        flat_inputs, flat_scaled, old_weights, width, in_scale, out_scale
    )
    first_new = beta_one * first_moment[0] + (1.0 - beta_one) * gradient
    second_new = beta_two * second_moment[0] + (1.0 - beta_two) * gradient * gradient
    first_hat = first_new / (1.0 - beta_one**adam_step)
    second_hat = second_new / (1.0 - beta_two**adam_step)
    new_weights = old_weights - learn_rate * (
        first_hat / (jnp.sqrt(second_hat) + adam_eps) + decay_rate * old_weights
    )
    positions = jnp.arange(groups, dtype=jnp.int32)
    holder = jnp.sum(
        jnp.where(owner_plan[:, None] == positions[None, :], positions[:, None], 0), axis=0
    )
    rows_here, columns = new_weights.shape
    pieces = jnp.concatenate(
        [
            array.astype(jnp.bfloat16).reshape(groups, 1, rows_here // groups, columns)
            for array in (new_weights, first_new, second_new)
        ],
        axis=1,
    )
    spread = exchange(pieces, "expert")
    ordered = jnp.concatenate(
        [lax.dynamic_slice_in_dim(spread, holder[p], 1, axis=0) for p in range(groups)], axis=0
    )
    collected = exchange(ordered, "expert")
    next_targets = slot_targets(next_routes, CAP)
    next_pairs = jnp.repeat(next_inputs, topk_count, axis=0)
    send_next = jnp.repeat(dispatch_pairs(next_targets, next_pairs, CAP), split, axis=0)
    received = exchange(send_next, "expert")
    flat_rows = received.reshape(-1, D)
    partials, collected = (forward_by_tokens if by_tokens else forward_by_weights)(
        flat_rows, new_weights.astype(jnp.bfloat16), collected, width, in_scale, out_scale
    )
    relocated = [
        collected[:, at].reshape(1, rows_here, columns).astype(jnp.float32) for at in range(3)
    ]
    returned = exchange(partials.reshape(received.shape), "expert").reshape(-1, D)
    places = lax.broadcasted_iota(jnp.int32, (next_targets.shape[0], groups * CAP), 1)
    selector = (
        next_targets[:, None] == (places // (split * CAP)) * CAP + places % CAP
    ).astype(jnp.bfloat16)
    pair_sums = jnp.dot(selector, returned, preferred_element_type=jnp.float32)
    weighted = pair_sums * next_gates
    layer_output = jnp.sum(weighted.reshape(-1, topk_count, D), axis=1).astype(jnp.bfloat16)
    return (layer_output, relocated[0], relocated[1], relocated[2])


def solution(mesh):
    placed = (
        P(("dp", "expert"), None),
        P(("dp", "expert"), None),
        P(("dp", "expert"), None),
        P(("dp", "expert"), None),
        P(("dp", "expert"), None),
        P(("dp", "expert"), None),
        P(("dp", "expert"), None),
        P("expert", "dp", None),
        P("expert", "dp", None),
        P("expert", "dp", None),
        P(),
    )
    return jax.shard_map(
        shards,
        mesh=mesh,
        in_specs=placed,
        out_specs=(
            P(("dp", "expert"), None),
            P("expert", "dp", None),
            P("expert", "dp", None),
            P("expert", "dp", None),
        ),
        check_vma=False,
    )
```
